256 devices in a mesh: ctx: 64 (over x, z, core), dp: 4 (over y).
Axes of the slice: x: 4, y: 4, z: 8, core: 2. Of those that a mesh axis runs over, the one named last changes fastest.
Arguments:
- queries: bfloat16 [4, 8192, 2048], P('dp', 'ctx'), may hold values from -80 to 80
- query_direction: bfloat16 [4, 8192, 2048], P('dp', 'ctx'), may hold values from -12 to 12
- keys: bfloat16 [4, 8192, 512], P('dp', 'ctx'), may hold values from -4 to 4
- key_tangent: bfloat16 [4, 8192, 512], P('dp', 'ctx'), may hold values from -12 to 12
- values: bfloat16 [4, 8192, 512], P('dp', 'ctx'), may hold values from -6 to 6
- value_tangent: bfloat16 [4, 8192, 512], P('dp', 'ctx'), may hold values from -12 to 12
- layer_input: bfloat16 [4, 8192, 4096], P('dp', 'ctx'), may hold values from -16 to 16
- cotangent: bfloat16 [4, 8192, 2048], P('dp', 'ctx'), may hold values from -12 to 12
Outputs:
- attended: bfloat16 [4, 8192, 2048], P('dp', 'ctx')
- value_update: float32 [4096, 512], P(('ctx', 'dp'))
The draws below stay inside these ranges and needn't reach their ends.
All inputs are finite; a program needn't handle non-finite values.
Results may differ from the reference program's by a relative error of at most 0.022.
Values may be sent and summed in bfloat16 or wider, within the bound.
No kernel may reach another device: no remote copies, remote signals or barrier semaphores. Data moves between devices by JAX's collectives and lax.ppermute only.
A program may use at most 192 MiB of HBM per device.

```python
import math
import jax
import jax.numpy as jnp
from jax import lax

MODEL_WIDTH = 4096
QUERY_HEADS = 16
KEY_VALUE_HEADS = 4
HEAD_SIZE = 128
GROUP_HEADS = 4
SEQUENCE_LENGTH = 4096
TOKENS_PER_SHARD = 8192
N_DP = 4


def base_keys(key):
    return jnp.clip(jax.random.normal(jax.random.fold_in(key, 101), (N_DP, TOKENS_PER_SHARD, KEY_VALUE_HEADS * HEAD_SIZE), jnp.float32), -4.0, 4.0)


def rising_scale():
    position = (jnp.arange(TOKENS_PER_SHARD, dtype=jnp.int32) % SEQUENCE_LENGTH).astype(jnp.float32)
    return (1.0 + 2.0 * position / (SEQUENCE_LENGTH - 1))[None, :, None]


def draw_keys(key, part):
    shared_heads = base_keys(key)
    return shared_heads.astype(jnp.bfloat16)


def draw_queries(key, part):
    key = jax.random.fold_in(key, 2)
    drawn = jnp.clip(jax.random.normal(key, (N_DP, TOKENS_PER_SHARD, QUERY_HEADS * HEAD_SIZE), jnp.float32), -4.0, 4.0)
    return drawn.astype(jnp.bfloat16)


def draw_query_direction(key, part):
    key = jax.random.fold_in(key, 3)
    array_shape = (N_DP, TOKENS_PER_SHARD, QUERY_HEADS * HEAD_SIZE)
    drawn = jnp.clip(jax.random.normal(key, array_shape, jnp.float32), -4.0, 4.0)
    return (drawn * rising_scale()).astype(jnp.bfloat16)


def draw_key_tangent(key, part):
    key = jax.random.fold_in(key, 4)
    array_shape = (N_DP, TOKENS_PER_SHARD, KEY_VALUE_HEADS * HEAD_SIZE)
    drawn = jnp.clip(jax.random.normal(key, array_shape, jnp.float32), -4.0, 4.0)
    return (drawn * rising_scale()).astype(jnp.bfloat16)


def draw_value_tangent(key, part):
    key = jax.random.fold_in(key, 5)
    array_shape = (N_DP, TOKENS_PER_SHARD, KEY_VALUE_HEADS * HEAD_SIZE)
    drawn = jnp.clip(jax.random.normal(key, array_shape, jnp.float32), -4.0, 4.0)
    return (drawn * rising_scale()).astype(jnp.bfloat16)


def draw_cotangent(key, part):
    key = jax.random.fold_in(key, 6)
    array_shape = (N_DP, TOKENS_PER_SHARD, QUERY_HEADS * HEAD_SIZE)
    drawn = jnp.clip(jax.random.normal(key, array_shape, jnp.float32), -4.0, 4.0)
    return (drawn * rising_scale()).astype(jnp.bfloat16)


def spiked(values, own_key, source, target, parts, factor):
    owner, partner = [(jnp.arange(values.shape[dim]) // (values.shape[dim] // parts)).reshape([-1 if axis == dim else 1 for axis in range(values.ndim)]) for dim in (source, target)]
    chosen = jax.random.permutation(own_key, parts)[partner]
    strong = (owner == chosen) | (owner == (partner + parts // 2) % parts)
    return jnp.where(strong, factor * values, values)


def shard_levels(stream_key, shape, shards, low, largest):
    factor_of = 1.0
    for dim, blocks in shards:
        heights = jax.random.uniform(jax.random.fold_in(jax.random.fold_in(stream_key, 6), dim), (blocks,), jnp.float32, low / len(shards), largest / len(shards))
        factor_of = factor_of * jnp.repeat(jnp.exp(heights), shape[dim] // blocks).reshape((-1,) + (1,) * (len(shape) - 1 - dim))
    return factor_of


def bell_draw(own_key, dims, width, limit, cuts=(), held_as=jnp.bfloat16):
    values = jax.random.normal(own_key, dims, jnp.float32) * width
    if len(cuts) > 0:
        values = shard_levels(own_key, dims, cuts, -0.22, 0.18) * values
    return jnp.clip(values, min=-limit, max=limit).astype(held_as)


def bell_draw_with(key, extent, deviation, bound, shards, heavy, held_as=jnp.bfloat16):
    entries = deviation * jax.random.normal(key, extent, jnp.float32)
    if shards:
        entries = entries * shard_levels(key, extent, shards, -0.22, 0.18)
    return jnp.clip(spiked(entries, jax.random.fold_in(key, 3), *heavy), -bound, bound).astype(held_as)


def setup_inputs(seed: int = 0) -> dict:
    key_list = jax.random.split(jax.random.key(seed), 9)
    return {
        "queries": draw_queries(jax.random.fold_in(key_list[8], 71), 0),
        "query_direction": draw_query_direction(jax.random.fold_in(key_list[8], 71), 0),
        "keys": draw_keys(jax.random.fold_in(key_list[8], 71), 0),
        "key_tangent": draw_key_tangent(jax.random.fold_in(key_list[8], 71), 0),
        "values": bell_draw(key_list[4], (N_DP, TOKENS_PER_SHARD, KEY_VALUE_HEADS * HEAD_SIZE), 1.0, 6.0, ((0, 4), (1, 64))),
        "value_tangent": draw_value_tangent(jax.random.fold_in(key_list[8], 71), 0),
        "layer_input": bell_draw_with(key_list[6], (N_DP, TOKENS_PER_SHARD, MODEL_WIDTH), 1.0, 16.0, ((0, 4), (1, 64)), (1, 2, 64, 4.0)),
        "cotangent": draw_cotangent(jax.random.fold_in(key_list[8], 71), 0),
    }


def reference(queries, query_direction, keys, key_tangent, values, value_tangent, layer_input, cotangent):
    seq_count = N_DP * (TOKENS_PER_SHARD // SEQUENCE_LENGTH)

    def as_seqs(array):
        return array.reshape(seq_count, SEQUENCE_LENGTH, array.shape[-1])
    score_scale = 1.0 / math.sqrt(HEAD_SIZE)
    query_block = math.gcd(SEQUENCE_LENGTH, 512)

    def one_sequence(items):
        query_full, query_tangent_full, key_full, key_tangent_full, value_full, value_tangent_full, cotangent_full = items
        key_forward = key_full.astype(jnp.float32).reshape(SEQUENCE_LENGTH, KEY_VALUE_HEADS, HEAD_SIZE)
        key_tangent_forward = key_tangent_full.astype(jnp.float32).reshape(SEQUENCE_LENGTH, KEY_VALUE_HEADS, HEAD_SIZE)
        value_forward = value_full.astype(jnp.float32).reshape(SEQUENCE_LENGTH, KEY_VALUE_HEADS, HEAD_SIZE)
        value_tangent_forward = value_tangent_full.astype(jnp.float32).reshape(SEQUENCE_LENGTH, KEY_VALUE_HEADS, HEAD_SIZE)

        def one_block(start_offset):
            query_rows = lax.dynamic_slice_in_dim(query_full, start_offset, query_block, 0).astype(jnp.float32).reshape(query_block, KEY_VALUE_HEADS, GROUP_HEADS, HEAD_SIZE)
            query_tangent_rows = lax.dynamic_slice_in_dim(query_tangent_full, start_offset, query_block, 0).astype(jnp.float32).reshape(query_block, KEY_VALUE_HEADS, GROUP_HEADS, HEAD_SIZE)
            cotangent_rows = lax.dynamic_slice_in_dim(cotangent_full, start_offset, query_block, 0).astype(jnp.float32).reshape(query_block, KEY_VALUE_HEADS, GROUP_HEADS, HEAD_SIZE)
            row_pos = start_offset + jnp.arange(query_block, dtype=jnp.int32)
            col_pos = jnp.arange(SEQUENCE_LENGTH, dtype=jnp.int32)
            visible = col_pos[None, :] <= row_pos[:, None]
            scores = jnp.einsum('tkgd,skd->kgts', query_rows, key_forward) * score_scale
            score_tan = (jnp.einsum('tkgd,skd->kgts', query_tangent_rows, key_forward) + jnp.einsum('tkgd,skd->kgts', query_rows, key_tangent_forward)) * score_scale
            top = lax.optimization_barrier(jnp.max(jnp.where(visible, scores, -jnp.inf), axis=-1))
            weights = jnp.where(visible, jnp.exp(scores - top[..., None]), 0.0)
            total = lax.optimization_barrier(jnp.sum(weights, axis=-1))
            moved = weights * score_tan
            slope = lax.optimization_barrier(jnp.sum(moved, axis=-1))
            weights_b = lax.optimization_barrier(weights.astype(jnp.bfloat16)).astype(jnp.float32)
            moved_b = lax.optimization_barrier(moved.astype(jnp.bfloat16)).astype(jnp.float32)
            acc = jnp.einsum('kgts,skd->tkgd', weights_b, value_forward)
            acc_tan = jnp.einsum('kgts,skd->tkgd', moved_b, value_forward) + jnp.einsum('kgts,skd->tkgd', weights_b, value_tangent_forward)
            total_t = jnp.transpose(total, (2, 0, 1))[..., None]
            slope_t = jnp.transpose(slope, (2, 0, 1))[..., None]
            output = acc / total_t
            output_tangent_rows = acc_tan / total_t - slope_t / total_t * output
            return (output.reshape(query_block, QUERY_HEADS * HEAD_SIZE).astype(jnp.bfloat16), jnp.sum(output_tangent_rows * cotangent_rows))
        starts = jnp.arange(SEQUENCE_LENGTH // query_block, dtype=jnp.int32) * query_block
        outs, dots = lax.map(one_block, starts)
        norm = jnp.sum(jnp.square(query_tangent_full.astype(jnp.float32))) + jnp.sum(jnp.square(key_tangent_full.astype(jnp.float32))) + jnp.sum(jnp.square(value_tangent_full.astype(jnp.float32)))
        return (outs.reshape(SEQUENCE_LENGTH, QUERY_HEADS * HEAD_SIZE), jnp.sum(dots), norm)
    attended, derivative, tangent_norm = lax.map(one_sequence, (as_seqs(queries), as_seqs(query_direction), as_seqs(keys), as_seqs(key_tangent), as_seqs(values), as_seqs(value_tangent), as_seqs(cotangent)))
    block_count = SEQUENCE_LENGTH * (QUERY_HEADS + 2 * KEY_VALUE_HEADS) * HEAD_SIZE
    factor = derivative / ((tangent_norm / block_count + 1e-06) * SEQUENCE_LENGTH * math.sqrt(QUERY_HEADS * HEAD_SIZE))

    def add_sequence(running, items):
        weight, inputs, tangent = items
        product = jnp.dot(inputs.T, tangent, preferred_element_type=jnp.float32)
        return (running + weight * product, None)
    update_start = jnp.zeros((MODEL_WIDTH, KEY_VALUE_HEADS * HEAD_SIZE), jnp.float32)
    value_update, unused = lax.scan(add_sequence, update_start, (factor, as_seqs(layer_input), as_seqs(value_tangent)))
    return (attended.reshape(N_DP, TOKENS_PER_SHARD, QUERY_HEADS * HEAD_SIZE), value_update)
```

```python
import functools
import math

import jax
import jax.numpy as jnp
from jax import lax
from jax.experimental import pallas as pl
from jax.experimental.pallas import tpu as pltpu
from jax.sharding import Mesh, PartitionSpec as P

QUERY_HEADS = 16
KEY_VALUE_HEADS = 4
HEAD_SIZE = 128
GROUP_HEADS = 4
SEQUENCE_LENGTH = 4096
Z = 8
TOKENS = 128
SCALE = 1.0 / math.sqrt(HEAD_SIZE)
SCALE_LOG2 = SCALE * math.log2(math.e)
F32 = jnp.float32
BF16 = jnp.bfloat16
VMEM = pl.BlockSpec(memory_space=pltpu.VMEM)
NEVER = -1e30
ACROSS = (((1,), (1,)), ((), ()))


def shaped(shape, dtype):
    return jax.ShapeDtypeStruct(shape, dtype)


def call(kernel, outs, n_in, flops=0, bytes_accessed=0, aliases=None, vmem=24 << 20):
    return pl.pallas_call(
        kernel,
        out_shape=outs,
        in_specs=[VMEM] * n_in,
        out_specs=[VMEM] * len(outs),
        input_output_aliases=aliases or {},
        compiler_params=pltpu.CompilerParams(vmem_limit_bytes=vmem),
        cost_estimate=pl.CostEstimate(
            flops=flops, bytes_accessed=bytes_accessed, transcendentals=0
        ),
    )


def own_head():
    return 2 * lax.axis_index("h") + lax.axis_index("c")


def pack_keys(keys, key_tangent, values, value_tangent, *pieces):
    head = own_head()
    for k in range(4):
        lanes = pl.ds(pl.multiple_of((head ^ k) * HEAD_SIZE, HEAD_SIZE), HEAD_SIZE)
        pieces[k][0, :, 0:128] = keys[:, lanes]
        pieces[k][0, :, 128:256] = key_tangent[:, lanes]
        pieces[k][1, :, 0:128] = values[:, lanes]
        pieces[k][1, :, 128:256] = value_tangent[:, lanes]


def pack_queries(queries, query_direction, cotangent, key_tangent, value_tangent, *outs):
    head = own_head()
    for k in range(4):
        for g in range(4):
            start = (head ^ k) * 512 + g * HEAD_SIZE
            lanes = pl.ds(pl.multiple_of(start, HEAD_SIZE), HEAD_SIZE)
            outs[k][:, g * 256 : g * 256 + 128] = query_direction[:, lanes]
            outs[k][:, g * 256 + 128 : g * 256 + 256] = queries[:, lanes]
        lanes = pl.ds(pl.multiple_of((head ^ k) * 512, 512), 512)
        outs[4 + k][...] = cotangent[:, lanes]
    norm = (
        jnp.sum(jnp.square(query_direction[...].astype(F32)))
        + jnp.sum(jnp.square(key_tangent[...].astype(F32)))
        + jnp.sum(jnp.square(value_tangent[...].astype(F32)))
    )
    outs[8][...] = jnp.full((8, 128), norm, F32)


def pack_inputs(layer_input, own, other):
    h = lax.axis_index("h")
    for s in range(2):
        mine = pl.ds(pl.multiple_of(s * 2048 + h * 1024, 1024), 1024)
        theirs = pl.ds(pl.multiple_of(s * 2048 + (1 - h) * 1024, 1024), 1024)
        own[:, s * 1024 : (s + 1) * 1024] = layer_input[:, mine]
        other[:, s * 1024 : (s + 1) * 1024] = layer_input[:, theirs]


def absorb(qq, block, acc, stats, t, diagonal):
    def one_head(g, _):
        rows = pl.ds(pl.multiple_of(g * 256, 256), 256)
        both_q = qq[t, rows, :]
        both_k = block[:, 0].reshape(256, 256)
        both_v = block[:, 1].reshape(256, 256)
        scores = lax.dot_general(
            both_q[:, 128:], both_k[:, :128], ACROSS, preferred_element_type=F32
        )
        tangent = lax.dot_general(both_q, both_k, ACROSS, preferred_element_type=F32)
        if diagonal:
            c = lax.axis_index("c")
            r = lax.broadcasted_iota(jnp.int32, (256, 256), 0)
            k = lax.broadcasted_iota(jnp.int32, (256, 256), 1)
            r = jnp.bitwise_xor(r, c * 128)
            k = jnp.bitwise_xor(k, c * 128)
            scores = jnp.where(k <= r, scores, NEVER)
        held = stats[t, rows, :]
        top, total, slope = held[:, 0:1], held[:, 1:2], held[:, 2:3]
        new_top = jnp.maximum(top, jnp.max(scores, axis=1, keepdims=True))
        decay = jnp.exp2((top - new_top) * SCALE_LOG2)
        weights = jnp.exp2((scores - new_top) * SCALE_LOG2)
        moved = weights * tangent
        total = total * decay + jnp.sum(weights, axis=1, keepdims=True)
        slope = slope * decay + jnp.sum(moved, axis=1, keepdims=True) * SCALE
        weights_b = weights.astype(BF16)
        moved_b = moved.astype(BF16)
        plain = jnp.dot(weights_b, both_v, preferred_element_type=F32)
        turned = jnp.dot(moved_b, both_v[:, :128], preferred_element_type=F32)
        acc[t, rows, 0:128] = acc[t, rows, 0:128] * decay + plain[:, :128]
        acc[t, rows, 128:256] = (
            acc[t, rows, 128:256] * decay + plain[:, 128:] + turned * SCALE
        )
        lane = lax.broadcasted_iota(jnp.int32, (256, 128), 1)
        stats[t, rows, :] = jnp.where(
            lane == 0, new_top, jnp.where(lane == 1, total, slope)
        )
        return 0

    lax.fori_loop(0, GROUP_HEADS, one_head, 0, unroll=2)


def attend_first(q0, q1, q2, q3, block_a, block_b, qq, acc, stats):
    h = lax.axis_index("h")
    for k, piece in enumerate((q0, q1, q2, q3)):
        for g in range(4):
            at = g * 256 + (k & 1) * 128
            qq[k >> 1, at : at + 128, :] = piece[:, g * 256 : (g + 1) * 256]
    acc[...] = jnp.zeros_like(acc)
    lane = lax.broadcasted_iota(jnp.int32, (2, 1024, 128), 2)
    stats[...] = jnp.where(lane == 0, NEVER, 0.0)
    absorb(qq, block_a, acc, stats, 0, True)
    absorb(qq, block_b, acc, stats, 1, True)

    @pl.when(h == 1)
    def _():
        absorb(qq, block_b, acc, stats, 0, False)

    @pl.when(h == 0)
    def _():
        absorb(qq, block_a, acc, stats, 1, False)


def attend(arrivals, qq, acc_in, stats_in, *refs):
    del acc_in, stats_in
    blocks, (acc, stats) = refs[: len(arrivals)], refs[len(arrivals) :]
    h = lax.axis_index("h")
    z = lax.axis_index("z")
    for (half, hops), block in zip(arrivals, blocks):
        source = (z - hops + Z) % Z
        earlier = source < z
        for t in range(2):
            if t == half:
                visible = earlier
            else:
                visible = (h ^ t) == 1

            @pl.when(visible)
            def _(block=block, t=t):
                absorb(qq, block, acc, stats, t, False)


def finish(acc, stats, c0, c1, c2, c3, norm, a0, a1, a2, a3, sums):
    dot = jnp.zeros((128, 128), F32)
    for k, (cot, att) in enumerate(((c0, a0), (c1, a1), (c2, a2), (c3, a3))):
        for g in range(4):
            at = g * 256 + (k & 1) * 128
            rows = slice(at, at + 128)
            held = stats[k >> 1, rows, :]
            total, slope = held[:, 1:2], held[:, 2:3]
            inverse = 1.0 / total
            output = acc[k >> 1, rows, 0:128] * inverse
            tangent = acc[k >> 1, rows, 128:256] * inverse - slope * inverse * output
            lanes = slice(g * 128, (g + 1) * 128)
            att[:, lanes] = output.astype(BF16)
            dot += tangent * cot[:, lanes].astype(F32)
    lane = lax.broadcasted_iota(jnp.int32, (8, 128), 1)
    sums[...] = jnp.where(lane == 0, jnp.sum(dot), jnp.where(lane == 1, norm[...], 0.0))


def place(r0, r1, r2, r3, out):
    head = own_head()
    for k, piece in enumerate((r0, r1, r2, r3)):
        lanes = pl.ds(pl.multiple_of((head ^ k) * 512, 512), 512)
        out[:, lanes] = piece[...]


def project(x0, x1, v0, v1, own, other):
    first = lax.axis_index("c") == 0
    tangent = jnp.concatenate([v0[...], v1[...]], axis=0)
    for s in range(2):
        for z in range(Z):
            lanes = slice(s * 1024 + z * 128, s * 1024 + (z + 1) * 128)
            rows = jnp.concatenate([x0[:, lanes], x1[:, lanes]], axis=0)
            product = lax.dot_general(
                rows, tangent, (((0,), (0,)), ((), ())), preferred_element_type=F32
            )
            top, bottom = product[:64], product[64:]
            own[z, s * 64 : (s + 1) * 64, :] = jnp.where(first, top, bottom)
            other[z, s * 64 : (s + 1) * 64, :] = jnp.where(first, bottom, top).astype(BF16)


def swap(array, k):
    return lax.ppermute(array, ("h", "c"), [(i, i ^ k) for i in range(4)])


def per_device(
    queries, query_direction, keys, key_tangent, values, value_tangent, layer_input, cotangent
):
    queries, query_direction, cotangent = queries[0], query_direction[0], cotangent[0]
    keys, key_tangent, values, value_tangent = keys[0], key_tangent[0], values[0], value_tangent[0]
    layer_input = layer_input[0]

    piece = shaped((2, TOKENS, 256), BF16)
    kv = call(pack_keys, [piece] * 4, 4)(keys, key_tangent, values, value_tangent)
    kv = [kv[0]] + [swap(kv[k], k) for k in (1, 2, 3)]
    block_a = jnp.stack([kv[0], kv[1]])
    block_b = jnp.stack([kv[2], kv[3]])

    packed = call(
        pack_queries,
        [shaped((TOKENS, 1024), BF16)] * 4
        + [shaped((TOKENS, 512), BF16)] * 4
        + [shaped((8, 128), F32)],
        5,
    )(queries, query_direction, cotangent, key_tangent, value_tangent)
    q_pieces = [packed[0]] + [swap(packed[k], k) for k in (1, 2, 3)]
    cot_pieces = [packed[4]] + [swap(packed[4 + k], k) for k in (1, 2, 3)]
    norm = packed[8]

    x_own, x_other = call(pack_inputs, [shaped((TOKENS, 2048), BF16)] * 2, 1)(layer_input)
    x_other = swap(x_other, 2)
    tangent_other = swap(value_tangent, 2)

    tile_flops = 2 * 6 * 128 * 256 * 1024
    state = [shaped((2, 1024, 256), F32), shaped((2, 1024, 128), F32)]
    qq, acc, stats = call(
        attend_first, [shaped((2, 1024, 256), BF16)] + state, 6, flops=3 * tile_flops
    )(*q_pieces, block_a, block_b)

    up = [(i, (i + 1) % Z) for i in range(Z)]
    down = [(i, (i - 1) % Z) for i in range(Z)]
    a_up = a_down = block_a
    b_up = b_down = block_b
    for k in range(1, 5):
        if k < 4:
            a_up = lax.ppermute(a_up, "z", up)
            a_down = lax.ppermute(a_down, "z", down)
            b_up = lax.ppermute(b_up, "z", up)
            b_down = lax.ppermute(b_down, "z", down)
            arrivals = ((0, k), (0, -k), (1, k), (1, -k))
            blocks = (a_up, a_down, b_up, b_down)
        else:
            a_up = lax.ppermute(a_up, "z", up)
            b_down = lax.ppermute(b_down, "z", down)
            arrivals = ((0, k), (1, -k))
            blocks = (a_up, b_down)
        acc, stats = call(
            functools.partial(attend, arrivals),
            state,
            3 + len(blocks),
            flops=3 * tile_flops * len(blocks) // 4,
            aliases={1: 0, 2: 1},
        )(qq, acc, stats, *blocks)

    *att, sums = call(
        finish, [shaped((TOKENS, 512), BF16)] * 4 + [shaped((8, 128), F32)], 7
    )(acc, stats, *cot_pieces, norm)
    att = [att[0]] + [swap(att[k], k) for k in (1, 2, 3)]
    (attended,) = call(place, [shaped((TOKENS, 2048), BF16)], 4)(*att)

    own, other = call(
        project,
        [shaped((Z, 128, 512), F32), shaped((Z, 128, 512), BF16)],
        4,
        flops=2 * 256 * 2048 * 512,
    )(x_own, x_other, value_tangent, tangent_other)
    pair = (own + swap(other, 1).astype(F32)).astype(BF16)
    parts = lax.all_to_all(pair, "z", 0, 0, tiled=True)
    product = jnp.sum(parts.astype(F32), axis=0)

    every = lax.all_to_all(
        jnp.broadcast_to(sums[:1], (4 * Z, 128)), ("h", "z", "c"), 0, 0, tiled=True
    )
    derivative, tangent_norm = jnp.sum(every[:, 0]), jnp.sum(every[:, 1])
    block_count = SEQUENCE_LENGTH * (QUERY_HEADS + 2 * KEY_VALUE_HEADS) * HEAD_SIZE
    factor = derivative / (
        (tangent_norm / block_count + 1e-06)
        * SEQUENCE_LENGTH
        * math.sqrt(QUERY_HEADS * HEAD_SIZE)
    )
    shares = lax.all_to_all(factor * product, ("s", "y"), 0, 0, tiled=True)
    value_update = jnp.sum(shares.reshape(8, 16, 512), axis=0)
    return attended[None], value_update


def solution(mesh):
    n_dp = mesh.shape["dp"]
    fine = Mesh(mesh.devices.reshape(2, 2, Z, 2, n_dp), ("s", "h", "z", "c", "y"))
    along = ("s", "h", "z", "c")
    placed = P("y", along, None)
    return jax.shard_map(
        per_device,
        mesh=fine,
        in_specs=(placed,) * 8,
        out_specs=(placed, P(along + ("y",), None)),
        check_vma=False,
    )
```

```python
import functools
import math

import jax
import jax.numpy as jnp
from jax import lax
from jax.experimental import pallas as pl
from jax.experimental.pallas import tpu as pltpu
from jax.sharding import Mesh, PartitionSpec as P

QUERY_HEADS = 16
KEY_VALUE_HEADS = 4
HEAD_SIZE = 128
GROUP_HEADS = 4
SEQUENCE_LENGTH = 4096
Z = 8
TOKENS = 128
SCALE = 1.0 / math.sqrt(HEAD_SIZE)
SCALE_LOG2 = SCALE * math.log2(math.e)
F32 = jnp.float32
BF16 = jnp.bfloat16
VMEM = pl.BlockSpec(memory_space=pltpu.VMEM)
ANY = pl.BlockSpec(memory_space=pl.ANY)
NEVER = -1e30
ACROSS = (((1,), (1,)), ((), ()))


def shaped(shape, dtype):
    return jax.ShapeDtypeStruct(shape, dtype)


def call(kernel, outs, ins, flops=0, scratch=(), out_specs=None, aliases=None, moved=0):
    return pl.pallas_call(
        kernel,
        out_shape=outs,
        in_specs=ins,
        out_specs=out_specs or [VMEM] * len(outs),
        scratch_shapes=list(scratch),
        input_output_aliases=aliases or {},
        compiler_params=pltpu.CompilerParams(vmem_limit_bytes=24 << 20),
        cost_estimate=pl.CostEstimate(flops=flops, bytes_accessed=moved, transcendentals=0),
    )


def copy_all(pairs, semaphores):
    copies = [
        pltpu.make_async_copy(source, target, semaphores.at[i])
        for i, (source, target) in enumerate(pairs)
    ]
    for copy in copies:
        copy.start()
    return copies


def own_head():
    return 2 * lax.axis_index("h") + lax.axis_index("c")


def pack_keys(keys, key_tangent, values, value_tangent, *refs):
    pieces, (held, semaphores) = refs[:4], refs[4:]
    head = own_head()
    sources = (keys, key_tangent, values, value_tangent)
    for copy in copy_all([(source, held.at[i]) for i, source in enumerate(sources)], semaphores):
        copy.wait()
    for k in range(4):
        lanes = pl.ds(pl.multiple_of((head ^ k) * HEAD_SIZE, HEAD_SIZE), HEAD_SIZE)
        pieces[k][:, 0:128] = held[0, :, lanes]
        pieces[k][:, 128:256] = held[1, :, lanes]
        pieces[k][:, 256:384] = held[2, :, lanes].T
        pieces[k][:, 384:512] = held[3, :, lanes].T


def pack_queries(queries, query_direction, q, semaphores):
    pairs = []
    for j in range(4):
        for g in range(4):
            lanes = pl.ds(j * 512 + g * 128, 128)
            pairs.append((query_direction.at[:, lanes], q.at[j, :, pl.ds(g * 256, 128)]))
            pairs.append((queries.at[:, lanes], q.at[j, :, pl.ds(g * 256 + 128, 128)]))
    for copy in copy_all(pairs, semaphores):
        copy.wait()


def pack_inputs(layer_input, value_tangent, cotangent, out, c0, c1, c2, c3, semaphores):
    head = own_head()
    pairs = []
    for h in range(2):
        for s in range(2):
            pairs.append(
                (
                    layer_input.at[:, pl.ds(s * 2048 + h * 1024, 1024)],
                    out.at[h, :, pl.ds(s * 1024, 1024)],
                )
            )
        pairs.append((value_tangent, out.at[h, :, pl.ds(2048, 512)]))
    for k, piece in enumerate((c0, c1, c2, c3)):
        lanes = pl.ds(pl.multiple_of((head ^ k) * 512, 512), 512)
        pairs.append((cotangent.at[:, lanes], piece))
    for copy in copy_all(pairs, semaphores):
        copy.wait()


def square_norm(query_direction, key_tangent, value_tangent, out):
    norm = (
        jnp.sum(jnp.square(query_direction[...].astype(F32)))
        + jnp.sum(jnp.square(key_tangent[...].astype(F32)))
        + jnp.sum(jnp.square(value_tangent[...].astype(F32)))
    )
    out[...] = jnp.full((8, 128), norm, F32)


def absorb(qq, block, acc, stats, t, diagonal):
    def two_heads(i, _):
        rows = pl.ds(pl.multiple_of(i * 512, 512), 512)
        both_q = qq[t, rows, :]
        both_k = block[:, :, 0:256].reshape(256, 256)
        value = jnp.concatenate([block[0, :, 256:384], block[1, :, 256:384]], axis=1)
        value_tan = jnp.concatenate([block[0, :, 384:512], block[1, :, 384:512]], axis=1)
        scores = lax.dot_general(
            both_k[:, :128], both_q[:, 128:], ACROSS, preferred_element_type=F32
        )
        tangent = lax.dot_general(both_k, both_q, ACROSS, preferred_element_type=F32)
        if diagonal:
            c = lax.axis_index("c")
            k = lax.broadcasted_iota(jnp.int32, (256, 512), 0)
            r = lax.broadcasted_iota(jnp.int32, (256, 512), 1) % 256
            k = jnp.bitwise_xor(k, c * 128)
            r = jnp.bitwise_xor(r, c * 128)
            scores = jnp.where(k <= r, scores, NEVER)
        top, total, slope = (stats[t, n : n + 1, rows] for n in range(3))
        new_top = jnp.maximum(top, jnp.max(scores, axis=0, keepdims=True))
        decay = jnp.exp2((top - new_top) * SCALE_LOG2)
        weights = jnp.exp2((scores - new_top) * SCALE_LOG2)
        moved = weights * tangent
        stats[t, 0:1, rows] = new_top
        stats[t, 1:2, rows] = total * decay + jnp.sum(weights, axis=0, keepdims=True)
        stats[t, 2:3, rows] = slope * decay + jnp.sum(moved, axis=0, keepdims=True) * SCALE
        weights_b = weights.astype(BF16)
        moved_b = moved.astype(BF16)
        both_v = jnp.concatenate([value, value_tan], axis=0)
        plain = jnp.dot(both_v, weights_b, preferred_element_type=F32)
        turned = jnp.dot(value, moved_b, preferred_element_type=F32)
        acc[t, 0:128, rows] = acc[t, 0:128, rows] * decay + plain[:128]
        acc[t, 128:256, rows] = (
            acc[t, 128:256, rows] * decay + plain[128:] + turned * SCALE
        )
        return 0

    lax.fori_loop(0, 2, two_heads, 0, unroll=2)


def attend_first(q, block_a, block_b, qq, acc, stats, q_held, held, semaphores):
    h, head = lax.axis_index("h"), own_head()
    copies = copy_all(
        [(q, q_held), (block_a, held.at[0]), (block_b, held.at[1])], semaphores
    )
    acc[...] = jnp.zeros_like(acc)
    line = lax.broadcasted_iota(jnp.int32, (2, 8, 1024), 1)
    stats[...] = jnp.where(line == 0, NEVER, 0.0)
    for copy in copies:
        copy.wait()
    for k in range(4):
        for g in range(4):
            at = g * 256 + (k & 1) * 128
            qq[k >> 1, at : at + 128, :] = q_held[head ^ k, :, g * 256 : (g + 1) * 256]
    absorb(qq, held.at[0], acc, stats, 0, True)
    absorb(qq, held.at[1], acc, stats, 1, True)

    @pl.when(h == 1)
    def _():
        absorb(qq, held.at[1], acc, stats, 0, False)

    @pl.when(h == 0)
    def _():
        absorb(qq, held.at[0], acc, stats, 1, False)


def attend(arrivals, qq, acc_in, stats_in, *refs):
    del acc_in, stats_in
    blocks, (acc, stats, held, semaphores) = refs[: len(arrivals)], refs[len(arrivals) :]
    h = lax.axis_index("h")
    z = lax.axis_index("z")
    copies = copy_all([(block, held.at[i]) for i, block in enumerate(blocks)], semaphores)
    for i, (half, hops) in enumerate(arrivals):
        copies[i].wait()
        source = (z - hops + Z) % Z
        earlier = source < z
        for t in range(2):
            if t == half:
                visible = earlier
            else:
                visible = (h ^ t) == 1

            @pl.when(visible)
            def _(i=i, t=t):
                absorb(qq, held.at[i], acc, stats, t, False)


def finish(acc, stats, c0, c1, c2, c3, norm, a0, a1, a2, a3, sums):
    dot = jnp.zeros((128, 128), F32)
    for k, (cot, att) in enumerate(((c0, a0), (c1, a1), (c2, a2), (c3, a3))):
        for g in range(4):
            at = g * 256 + (k & 1) * 128
            rows = slice(at, at + 128)
            total, slope = stats[k >> 1, 1:2, rows], stats[k >> 1, 2:3, rows]
            inverse = 1.0 / total
            output = acc[k >> 1, 0:128, rows] * inverse
            tangent = acc[k >> 1, 128:256, rows] * inverse - slope * inverse * output
            lanes = slice(g * 128, (g + 1) * 128)
            att[:, lanes] = output.T.astype(BF16)
            dot += tangent.T * cot[:, lanes].astype(F32)
    lane = lax.broadcasted_iota(jnp.int32, (8, 128), 1)
    sums[...] = jnp.where(lane == 0, jnp.sum(dot), jnp.where(lane == 1, norm[...], 0.0))


def place(r0, r1, r2, r3, out):
    head = own_head()
    for k, piece in enumerate((r0, r1, r2, r3)):
        lanes = pl.ds(pl.multiple_of((head ^ k) * 512, 512), 512)
        out[:, lanes] = piece[...]


def project(x, own, other):
    first = lax.axis_index("c") == 0
    tangent = jnp.concatenate([x[0, :, 2048:2560], x[1, :, 2048:2560]], axis=0)
    for s in range(2):
        for z in range(Z):
            lanes = slice(s * 1024 + z * 128, s * 1024 + (z + 1) * 128)
            rows = jnp.concatenate([x[0, :, lanes], x[1, :, lanes]], axis=0)
            product = lax.dot_general(
                rows, tangent, (((0,), (0,)), ((), ())), preferred_element_type=F32
            )
            top, bottom = product[:64], product[64:]
            own[z, s * 64 : (s + 1) * 64, :] = jnp.where(first, top, bottom)
            other[z, s * 64 : (s + 1) * 64, :] = jnp.where(first, bottom, top).astype(BF16)


def after(array, *others):
    return lax.optimization_barrier((array,) + others)[0]


def swap(array, k):
    return lax.ppermute(array, ("h", "c"), [(i, i ^ k) for i in range(4)])


def per_device(
    queries, query_direction, keys, key_tangent, values, value_tangent, layer_input, cotangent
):
    queries, query_direction, cotangent = queries[0], query_direction[0], cotangent[0]
    keys, key_tangent, values, value_tangent = keys[0], key_tangent[0], values[0], value_tangent[0]
    layer_input = layer_input[0]

    dma = pltpu.SemaphoreType.DMA
    piece = shaped((TOKENS, 512), BF16)
    kv = call(
        pack_keys,
        [piece] * 4,
        [ANY] * 4,
        scratch=[pltpu.VMEM((4, TOKENS, 512), BF16), dma((4,))],
    )(keys, key_tangent, values, value_tangent)
    kv1, kv2, kv3 = [swap(kv[k], k) for k in (1, 2, 3)]
    block_a = jnp.stack([kv[0], kv1])
    block_b = jnp.stack([kv2, kv3])

    (q_all,) = call(
        pack_queries,
        [shaped((4, TOKENS, 1024), BF16)],
        [ANY] * 2,
        out_specs=[ANY],
        scratch=[dma((32,))],
    )(after(queries, kv[0]), query_direction)
    q_all = lax.all_to_all(after(q_all, kv2, kv3), ("h", "c"), 0, 0, tiled=True)
    x_all, *cot = call(
        pack_inputs,
        [shaped((2, TOKENS, 2560), BF16)] + [shaped((TOKENS, 512), BF16)] * 4,
        [ANY] * 3,
        out_specs=[ANY] * 5,
        scratch=[dma((10,))],
    )(after(layer_input, block_b), value_tangent, cotangent)
    (norm,) = call(square_norm, [shaped((8, 128), F32)], [VMEM] * 3)(
        after(query_direction, x_all), key_tangent, value_tangent
    )

    tile_flops = 2 * 6 * 128 * 256 * 1024
    state = [shaped((2, 256, 1024), F32), shaped((2, 8, 1024), F32)]
    up = [(i, (i + 1) % Z) for i in range(Z)]
    down = [(i, (i - 1) % Z) for i in range(Z)]

    def hop(array, route):
        return lax.ppermute(array, "z", route)

    def attend_step(acc, stats, arrivals, blocks):
        return call(
            functools.partial(attend, arrivals),
            state,
            [VMEM] * 3 + [ANY] * len(blocks),
            flops=3 * tile_flops * len(blocks) // 4,
            scratch=[pltpu.VMEM((len(blocks), 2, TOKENS, 512), BF16), dma((len(blocks),))],
            aliases={1: 0, 2: 1},
        )(qq, acc, stats, *blocks)

    def arrivals_of(k):
        return ((0, k), (0, -k), (1, k), (1, -k))

    ring1 = (hop(block_a, up), hop(block_a, down), hop(block_b, up), hop(block_b, down))
    q_all, *ring1 = lax.optimization_barrier((q_all, *ring1))
    ring2 = [hop(ring1[i], (up, down)[i % 2]) for i in range(4)]
    x_all = lax.all_to_all(after(x_all, q_all), "h", 0, 0, tiled=True)
    qq, acc, stats = call(
        attend_first,
        [shaped((2, 1024, 256), BF16)] + state,
        [ANY] * 3,
        flops=3 * tile_flops,
        scratch=[
            pltpu.VMEM((4, TOKENS, 1024), BF16),
            pltpu.VMEM((2, 2, TOKENS, 512), BF16),
            dma((3,)),
        ],
    )(q_all, block_a, block_b)
    acc, stats = attend_step(acc, stats, arrivals_of(1), ring1)
    stats, x_all, *ring2 = lax.optimization_barrier((stats, x_all, *ring2))
    ring3 = [hop(ring2[i], (up, down)[i % 2]) for i in range(4)]
    own, other = call(
        project,
        [shaped((Z, 128, 512), F32), shaped((Z, 128, 512), BF16)],
        [VMEM],
        flops=2 * 256 * 2048 * 512,
    )(x_all)
    acc, stats = attend_step(acc, stats, arrivals_of(2), ring2)
    other, stats, norm, *ring3 = lax.optimization_barrier((other, stats, norm, *ring3))
    ring4 = [hop(ring3[0], up), hop(ring3[3], down)]
    pair = (own + swap(other, 1).astype(F32)).astype(BF16)
    cot = [cot[0]] + [swap(after(cot[k], stats), k) for k in (1, 2, 3)]
    acc, stats = attend_step(acc, stats, arrivals_of(3), ring3)
    stats, pair, *ring4 = lax.optimization_barrier((stats, pair, *ring4))
    parts = lax.all_to_all(pair, "z", 0, 0, tiled=True)
    acc, stats = attend_step(acc, stats, ((0, 4), (1, -4)), ring4)

    *att, sums = call(
        finish, [shaped((TOKENS, 512), BF16)] * 4 + [shaped((8, 128), F32)], [VMEM] * 7
    )(acc, stats, *cot, norm)
    att = [att[0]] + [swap(att[k], k) for k in (1, 2, 3)]
    (attended,) = call(place, [shaped((TOKENS, 2048), BF16)], [VMEM] * 4)(*att)

    for axis, size, bit in (("c", 2, 1), ("z", Z, 1), ("z", Z, 2), ("z", Z, 4), ("h", 2, 1)):
        sums = sums + lax.ppermute(sums, axis, [(i, i ^ bit) for i in range(size)])
    derivative, tangent_norm = sums[0, 0], sums[0, 1]
    product = jnp.sum(after(parts, sums).astype(F32), axis=0)
    block_count = SEQUENCE_LENGTH * (QUERY_HEADS + 2 * KEY_VALUE_HEADS) * HEAD_SIZE
    factor = derivative / (
        (tangent_norm / block_count + 1e-06)
        * SEQUENCE_LENGTH
        * math.sqrt(QUERY_HEADS * HEAD_SIZE)
    )
    shares = lax.all_to_all(factor * product, ("s", "y"), 0, 0, tiled=True)
    value_update = jnp.sum(shares.reshape(8, 16, 512), axis=0)
    return attended[None], value_update


def solution(mesh):
    n_dp = mesh.shape["dp"]
    fine = Mesh(mesh.devices.reshape(2, 2, Z, 2, n_dp), ("s", "h", "z", "c", "y"))
    along = ("s", "h", "z", "c")
    placed = P("y", along, None)
    return jax.shard_map(
        per_device,
        mesh=fine,
        in_specs=(placed,) * 8,
        out_specs=(placed, P(along + ("y",), None)),
        check_vma=False,
    )
```

```python
import functools
import math

import jax
import jax.numpy as jnp
from jax import lax
from jax.experimental import pallas as pl
from jax.experimental.pallas import tpu as pltpu
from jax.sharding import Mesh, PartitionSpec as P

QUERY_HEADS = 16
KEY_VALUE_HEADS = 4
HEAD_SIZE = 128
GROUP_HEADS = 4
SEQUENCE_LENGTH = 4096
Z = 8
TOKENS = 128
SCALE = 1.0 / math.sqrt(HEAD_SIZE)
SCALE_LOG2 = SCALE * math.log2(math.e)
F32 = jnp.float32
BF16 = jnp.bfloat16
VMEM = pl.BlockSpec(memory_space=pltpu.VMEM)
ANY = pl.BlockSpec(memory_space=pltpu.HBM)
NEVER = -1e30
LARGE = 60 << 20
ACROSS = (((1,), (1,)), ((), ()))


def shaped(shape, dtype):
    return jax.ShapeDtypeStruct(shape, dtype)


def call(kernel, outs, ins, flops=0, scratch=(), out_specs=None, aliases=None, vmem=24 << 20):
    return pl.pallas_call(
        kernel,
        out_shape=outs,
        in_specs=ins,
        out_specs=out_specs or [VMEM] * len(outs),
        scratch_shapes=list(scratch),
        input_output_aliases=aliases or {},
        compiler_params=pltpu.CompilerParams(vmem_limit_bytes=vmem),
        cost_estimate=pl.CostEstimate(flops=flops, bytes_accessed=0, transcendentals=0),
    )


def copy_all(pairs, semaphores):
    copies = [
        pltpu.make_async_copy(source, target, semaphores.at[i])
        for i, (source, target) in enumerate(pairs)
    ]
    for copy in copies:
        copy.start()
    return copies


def own_head():
    return 2 * lax.axis_index("h") + lax.axis_index("c")


def pack_keys(keys, key_tangent, values, value_tangent, *refs):
    pieces, (held, semaphores) = refs[:4], refs[4:]
    head = own_head()
    sources = (keys, key_tangent, values, value_tangent)
    for copy in copy_all([(source, held.at[i]) for i, source in enumerate(sources)], semaphores):
        copy.wait()
    for k in range(4):
        lanes = pl.ds(pl.multiple_of((head ^ k) * HEAD_SIZE, HEAD_SIZE), HEAD_SIZE)
        pieces[k][:, 0:128] = held[0, :, lanes]
        pieces[k][:, 128:256] = held[1, :, lanes]
        pieces[k][:, 256:384] = held[2, :, lanes].T
        pieces[k][:, 384:512] = held[3, :, lanes].T


def pack_queries(queries, query_direction, q, semaphores):
    pairs = []
    for j in range(4):
        for g in range(4):
            lanes = pl.ds(j * 512 + g * 128, 128)
            pairs.append((query_direction.at[:, lanes], q.at[j, :, pl.ds(g * 256, 128)]))
            pairs.append((queries.at[:, lanes], q.at[j, :, pl.ds(g * 256 + 128, 128)]))
    for copy in copy_all(pairs, semaphores):
        copy.wait()


def pack_inputs(layer_input, value_tangent, cotangent, own, other, c0, c1, c2, c3, semaphores):
    h, head = lax.axis_index("h"), own_head()
    pairs = []
    for s in range(2):
        for target, half in ((own, h), (other, 1 - h)):
            lanes = pl.ds(pl.multiple_of(s * 2048 + half * 1024, 1024), 1024)
            pairs.append((layer_input.at[:, lanes], target.at[:, pl.ds(s * 1024, 1024)]))
    for target in (own, other):
        pairs.append((value_tangent, target.at[:, pl.ds(2048, 512)]))
    for k, piece in enumerate((c0, c1, c2, c3)):
        lanes = pl.ds(pl.multiple_of((head ^ k) * 512, 512), 512)
        pairs.append((cotangent.at[:, lanes], piece))
    for copy in copy_all(pairs, semaphores):
        copy.wait()


def square_norm(query_direction, key_tangent, value_tangent, out):
    norm = (
        jnp.sum(jnp.square(query_direction[...].astype(F32)))
        + jnp.sum(jnp.square(key_tangent[...].astype(F32)))
        + jnp.sum(jnp.square(value_tangent[...].astype(F32)))
    )
    out[...] = jnp.full((8, 128), norm, F32)


def absorb(qq, blocks, acc, stats, t, diagonal):
    def two_heads(i, _):
        rows = pl.ds(pl.multiple_of(i * 512, 512), 512)
        both_q = qq[t, rows, :]
        halves = [(block, i) for block in blocks for i in range(2)]
        both_k = jnp.concatenate([block[i, :, 0:256] for block, i in halves], axis=0)
        value = jnp.concatenate([block[i, :, 256:384] for block, i in halves], axis=1)
        value_tan = jnp.concatenate([block[i, :, 384:512] for block, i in halves], axis=1)
        scores = lax.dot_general(
            both_k[:, :128], both_q[:, 128:], ACROSS, preferred_element_type=F32
        )
        tangent = lax.dot_general(both_k, both_q, ACROSS, preferred_element_type=F32)
        if diagonal:
            c = lax.axis_index("c")
            k = lax.broadcasted_iota(jnp.int32, (256, 512), 0)
            r = lax.broadcasted_iota(jnp.int32, (256, 512), 1) % 256
            k = jnp.bitwise_xor(k, c * 128)
            r = jnp.bitwise_xor(r, c * 128)
            scores = jnp.where(k <= r, scores, NEVER)
        top, total, slope = (stats[t, n : n + 1, rows] for n in range(3))
        new_top = jnp.maximum(top, jnp.max(scores, axis=0, keepdims=True))
        decay = jnp.exp2((top - new_top) * SCALE_LOG2)
        weights = jnp.exp2((scores - new_top) * SCALE_LOG2)
        moved = weights * tangent
        stats[t, 0:1, rows] = new_top
        stats[t, 1:2, rows] = total * decay + jnp.sum(weights, axis=0, keepdims=True)
        stats[t, 2:3, rows] = slope * decay + jnp.sum(moved, axis=0, keepdims=True) * SCALE
        weights_b = weights.astype(BF16)
        moved_b = moved.astype(BF16)
        both_v = jnp.concatenate([value, value_tan], axis=0)
        plain = jnp.dot(both_v, weights_b, preferred_element_type=F32)
        turned = jnp.dot(value, moved_b, preferred_element_type=F32)
        acc[t, 0:128, rows] = acc[t, 0:128, rows] * decay + plain[:128]
        acc[t, 128:256, rows] = (
            acc[t, 128:256, rows] * decay + plain[128:] + turned * SCALE
        )
        return 0

    lax.fori_loop(0, 2, two_heads, 0, unroll=2)


def attend_first(q, block_a, block_b, qq, acc, stats, q_held, held, semaphores):
    h, head = lax.axis_index("h"), own_head()
    copies = copy_all(
        [(q, q_held), (block_a, held.at[0]), (block_b, held.at[1])], semaphores
    )
    acc[...] = jnp.zeros_like(acc)
    line = lax.broadcasted_iota(jnp.int32, (2, 8, 1024), 1)
    stats[...] = jnp.where(line == 0, NEVER, 0.0)
    for copy in copies:
        copy.wait()
    for k in range(4):
        for g in range(4):
            at = g * 256 + (k & 1) * 128
            qq[k >> 1, at : at + 128, :] = q_held[head ^ k, :, g * 256 : (g + 1) * 256]
    absorb(qq, [held.at[0]], acc, stats, 0, True)
    absorb(qq, [held.at[1]], acc, stats, 1, True)

    @pl.when(h == 1)
    def _():
        absorb(qq, [held.at[1]], acc, stats, 0, False)

    @pl.when(h == 0)
    def _():
        absorb(qq, [held.at[0]], acc, stats, 1, False)


def attend(arrivals, qq, acc_in, stats_in, *refs):
    del acc_in, stats_in
    blocks, (acc, stats, held, semaphores) = refs[: len(arrivals)], refs[len(arrivals) :]
    h = lax.axis_index("h")
    z = lax.axis_index("z")
    copies = copy_all([(block, held.at[i]) for i, block in enumerate(blocks)], semaphores)
    earlier = [(z - hops + Z) % Z < z for _, hops in arrivals]
    for copy in copies:
        copy.wait()

    def absorb_when(visible, t, which):
        @pl.when(visible)
        def _():
            absorb(qq, [held.at[i] for i in which], acc, stats, t, False)

    first, second = arrivals[0][0], arrivals[1][0]
    if first == second:
        both = jnp.logical_and(earlier[0], earlier[1])
        absorb_when(both, first, (0, 1))
        absorb_when(jnp.logical_and(earlier[0], jnp.logical_not(both)), first, (0,))
        absorb_when(jnp.logical_and(earlier[1], jnp.logical_not(both)), first, (1,))
        absorb_when((h ^ (1 - first)) == 1, 1 - first, (0, 1))
    else:
        for i, half in enumerate((first, second)):
            absorb_when(earlier[i], half, (i,))
            absorb_when((h ^ (1 - half)) == 1, 1 - half, (i,))


def finish(acc, stats, c0, c1, c2, c3, norm, a0, a1, a2, a3, sums):
    dot = jnp.zeros((128, 128), F32)
    for k, (cot, att) in enumerate(((c0, a0), (c1, a1), (c2, a2), (c3, a3))):
        for g in range(4):
            at = g * 256 + (k & 1) * 128
            rows = slice(at, at + 128)
            total, slope = stats[k >> 1, 1:2, rows], stats[k >> 1, 2:3, rows]
            inverse = 1.0 / total
            output = acc[k >> 1, 0:128, rows] * inverse
            tangent = acc[k >> 1, 128:256, rows] * inverse - slope * inverse * output
            lanes = slice(g * 128, (g + 1) * 128)
            att[:, lanes] = output.T.astype(BF16)
            dot += tangent.T * cot[:, lanes].astype(F32)
    lane = lax.broadcasted_iota(jnp.int32, (8, 128), 1)
    sums[...] = jnp.where(lane == 0, jnp.sum(dot), jnp.where(lane == 1, norm[...], 0.0))


def place(r0, r1, r2, r3, out):
    head = own_head()
    for k, piece in enumerate((r0, r1, r2, r3)):
        lanes = pl.ds(pl.multiple_of((head ^ k) * 512, 512), 512)
        out[:, lanes] = piece[...]


def project(x0, x1, own, other):
    first = lax.axis_index("c") == 0
    tangent = jnp.concatenate([x0[:, 2048:2560], x1[:, 2048:2560]], axis=0)
    for s in range(2):
        for z in range(Z):
            lanes = slice(s * 1024 + z * 128, s * 1024 + (z + 1) * 128)
            rows = jnp.concatenate([x0[:, lanes], x1[:, lanes]], axis=0)
            product = lax.dot_general(
                rows, tangent, (((0,), (0,)), ((), ())), preferred_element_type=F32
            )
            top, bottom = product[:64], product[64:]
            mine = jnp.where(first, top, bottom)
            theirs = jnp.where(first, bottom, top).astype(BF16)
            for y in range(4):
                rows, taken = slice(z * 16, (z + 1) * 16), slice(y * 16, (y + 1) * 16)
                own[s * 4 + y, rows, :] = mine[taken]
                other[s * 4 + y, rows, :] = theirs[taken]


def after(array, *others):
    return lax.optimization_barrier((array,) + others)[0]


def swap(array, k):
    return lax.ppermute(array, ("h", "c"), [(i, i ^ k) for i in range(4)])


def per_device(
    queries, query_direction, keys, key_tangent, values, value_tangent, layer_input, cotangent
):
    queries, query_direction, cotangent = queries[0], query_direction[0], cotangent[0]
    keys, key_tangent, values, value_tangent = keys[0], key_tangent[0], values[0], value_tangent[0]
    layer_input = layer_input[0]

    dma = pltpu.SemaphoreType.DMA
    n_dp = lax.axis_size("y")
    piece = shaped((TOKENS, 512), BF16)
    kv = call(
        pack_keys,
        [piece] * 4,
        [ANY] * 4,
        scratch=[pltpu.VMEM((4, TOKENS, 512), BF16), dma((4,))],
        vmem=LARGE,
    )(keys, key_tangent, values, value_tangent)
    kv1, kv2, kv3 = [swap(kv[k], k) for k in (1, 2, 3)]
    block_a = jnp.stack([kv[0], kv1])
    block_b = jnp.stack([kv2, kv3])

    (q_all,) = call(
        pack_queries,
        [shaped((4, TOKENS, 1024), BF16)],
        [ANY] * 2,
        scratch=[dma((32,))],
        vmem=LARGE,
    )(after(queries, kv[0]), query_direction)
    q_all = lax.all_to_all(after(q_all, block_a, block_b), ("h", "c"), 0, 0, tiled=True)
    x_own, x_other, *cot = call(
        pack_inputs,
        [shaped((TOKENS, 2560), BF16)] * 2 + [shaped((TOKENS, 512), BF16)] * 4,
        [ANY] * 3,
        scratch=[dma((10,))],
        vmem=LARGE,
    )(after(layer_input, block_b), value_tangent, cotangent)
    (norm,) = call(square_norm, [shaped((8, 128), F32)], [VMEM] * 3)(
        after(query_direction, x_own), key_tangent, value_tangent
    )

    tile_flops = 2 * 6 * 128 * 256 * 1024
    state = [shaped((2, 256, 1024), F32), shaped((2, 8, 1024), F32)]
    up = [(i, (i + 1) % Z) for i in range(Z)]
    down = [(i, (i - 1) % Z) for i in range(Z)]

    def hop(array, route):
        return lax.ppermute(array, "z", route)

    def attend_step(acc, stats, arrivals, blocks):
        return call(
            functools.partial(attend, arrivals),
            state,
            [VMEM] * 3 + [ANY] * len(blocks),
            flops=3 * tile_flops * len(blocks) // 4,
            scratch=[pltpu.VMEM((len(blocks), 2, TOKENS, 512), BF16), dma((len(blocks),))],
            aliases={1: 0, 2: 1},
        )(qq, acc, stats, *blocks)

    def stage(blocks):
        return [hop(blocks[i], (up, down)[i % 2]) for i in range(4)]

    tie = lax.optimization_barrier
    ring1 = stage((block_a, block_a, block_b, block_b))
    *ring1, x_own, x_other = tie((*ring1, x_own, x_other))
    ring2 = stage(ring1)
    qq, acc, stats = call(
        attend_first,
        [shaped((2, 1024, 256), BF16)] + state,
        [ANY] * 3,
        flops=3 * tile_flops,
        scratch=[
            pltpu.VMEM((4, TOKENS, 1024), BF16),
            pltpu.VMEM((2, 2, TOKENS, 512), BF16),
            dma((3,)),
        ],
    )(q_all, block_a, block_b)
    x_other = swap(after(x_other, q_all), 2)
    acc, stats = attend_step(acc, stats, ((0, 1), (0, -1)), ring1[:2])
    *ring2, acc, stats, x_other, norm = tie((*ring2, acc, stats, x_other, norm))

    ring3 = stage(ring2)
    own, other = call(
        project,
        [shaped((Z, 128, 512), F32), shaped((Z, 128, 512), BF16)],
        [VMEM] * 2,
        flops=2 * 256 * 2048 * 512,
    )(x_own, x_other)
    acc, other = tie((acc, other))
    theirs = swap(other, 1)
    cot = [cot[0]] + [swap(after(cot[k], x_other), k) for k in (1, 2, 3)]
    acc, stats = attend_step(acc, stats, ((1, 1), (1, -1)), ring1[2:])
    acc, stats = attend_step(acc, stats, ((0, 2), (0, -2)), ring2[:2])
    ring3, acc, stats, theirs, cot = tie((ring3, acc, stats, theirs, cot))

    ring4 = [hop(ring3[0], up), hop(ring3[3], down)]
    pair = (own + theirs.astype(F32)).astype(BF16)
    acc, pair = tie((acc, pair))
    parts = lax.all_to_all(pair, ("s", "y"), 0, 0, tiled=True)
    acc, stats = attend_step(acc, stats, ((1, 2), (1, -2)), ring2[2:])
    acc, stats = attend_step(acc, stats, ((0, 3), (0, -3)), ring3[:2])
    ring4, acc, stats = tie((ring4, acc, stats))

    acc, stats = attend_step(acc, stats, ((1, 3), (1, -3)), ring3[2:])
    acc, stats = attend_step(acc, stats, ((0, 4), (1, -4)), ring4)
    acc = after(acc, parts)

    *att, sums = call(
        finish, [shaped((TOKENS, 512), BF16)] * 4 + [shaped((8, 128), F32)], [VMEM] * 7
    )(acc, stats, *cot, norm)
    sums = sums[:1] + swap(sums[:1], 1)
    att = [att[0]] + [swap(after(att[k], sums), k) for k in (1, 2, 3)]
    (attended,) = call(place, [shaped((TOKENS, 2048), BF16)], [VMEM] * 4)(*att)

    every = lax.all_to_all(
        jnp.broadcast_to(sums, (32 * n_dp, 128)), ("s", "h", "z", "y"), 0, 0, tiled=True
    )
    every = after(every, attended).reshape(2, 2 * Z, n_dp, 128).sum(axis=1)
    derivative, tangent_norm = every[..., 0], every[..., 1]
    block_count = SEQUENCE_LENGTH * (QUERY_HEADS + 2 * KEY_VALUE_HEADS) * HEAD_SIZE
    factor = derivative / (
        (tangent_norm / block_count + 1e-06)
        * SEQUENCE_LENGTH
        * math.sqrt(QUERY_HEADS * HEAD_SIZE)
    )
    shares = jnp.sum(factor.reshape(8, 1, 1) * parts.astype(F32), axis=0)
    shares = lax.all_to_all(shares, "z", 0, 0, tiled=True)
    value_update = jnp.sum(shares.reshape(Z, 16, 512), axis=0)
    return attended[None], value_update


def solution(mesh):
    n_dp = mesh.shape["dp"]
    fine = Mesh(mesh.devices.reshape(2, 2, Z, 2, n_dp), ("s", "h", "z", "c", "y"))
    along = ("s", "h", "z", "c")
    placed = P("y", along, None)
    return jax.shard_map(
        per_device,
        mesh=fine,
        in_specs=(placed,) * 8,
        out_specs=(placed, P(along + ("y",), None)),
        check_vma=False,
    )
```

```python
import functools
import math

import jax
import jax.numpy as jnp
from jax import lax
from jax.experimental import pallas as pl
from jax.experimental.pallas import tpu as pltpu
from jax.sharding import Mesh, PartitionSpec as P

QUERY_HEADS = 16
KEY_VALUE_HEADS = 4
HEAD_SIZE = 128
GROUP_HEADS = 4
SEQUENCE_LENGTH = 4096
Z = 8
TOKENS = 128
SCALE = 1.0 / math.sqrt(HEAD_SIZE)
SCALE_LOG2 = SCALE * math.log2(math.e)
F32 = jnp.float32
BF16 = jnp.bfloat16
VMEM = pl.BlockSpec(memory_space=pltpu.VMEM)
ANY = pl.BlockSpec(memory_space=pltpu.HBM)
NEVER = -1e30
LARGE = 60 << 20
ACROSS = (((1,), (1,)), ((), ()))


def shaped(shape, dtype):
    return jax.ShapeDtypeStruct(shape, dtype)


def call(kernel, outs, ins, flops=0, scratch=(), out_specs=None, aliases=None, vmem=24 << 20):
    return pl.pallas_call(
        kernel,
        out_shape=outs,
        in_specs=ins,
        out_specs=out_specs or [VMEM] * len(outs),
        scratch_shapes=list(scratch),
        input_output_aliases=aliases or {},
        compiler_params=pltpu.CompilerParams(vmem_limit_bytes=vmem),
        cost_estimate=pl.CostEstimate(flops=flops, bytes_accessed=0, transcendentals=0),
    )


def copy_all(pairs, semaphores):
    copies = [
        pltpu.make_async_copy(source, target, semaphores.at[i])
        for i, (source, target) in enumerate(pairs)
    ]
    for copy in copies:
        copy.start()
    return copies


def own_head():
    return 2 * lax.axis_index("h") + lax.axis_index("c")


def pack_keys(keys, key_tangent, values, value_tangent, *refs):
    pieces, (held, semaphores) = refs[:4], refs[4:]
    head = own_head()
    sources = (keys, key_tangent, values, value_tangent)
    for copy in copy_all([(source, held.at[i]) for i, source in enumerate(sources)], semaphores):
        copy.wait()
    for k in range(4):
        lanes = pl.ds(pl.multiple_of((head ^ k) * HEAD_SIZE, HEAD_SIZE), HEAD_SIZE)
        pieces[k][:, 0:128] = held[0, :, lanes]
        pieces[k][:, 128:256] = held[1, :, lanes]
        pieces[k][:, 256:384] = held[2, :, lanes].T
        pieces[k][:, 384:512] = held[3, :, lanes].T


def pack_queries(queries, query_direction, q, semaphores):
    pairs = []
    for j in range(4):
        for g in range(4):
            lanes = pl.ds(j * 512 + g * 128, 128)
            pairs.append((query_direction.at[:, lanes], q.at[j, :, pl.ds(g * 256, 128)]))
            pairs.append((queries.at[:, lanes], q.at[j, :, pl.ds(g * 256 + 128, 128)]))
    for copy in copy_all(pairs, semaphores):
        copy.wait()


def pack_inputs(layer_input, value_tangent, cotangent, own, other, c0, c1, c2, c3, semaphores):
    h, head = lax.axis_index("h"), own_head()
    pairs = []
    for s in range(2):
        for target, half in ((own, h), (other, 1 - h)):
            lanes = pl.ds(pl.multiple_of(s * 2048 + half * 1024, 1024), 1024)
            pairs.append((layer_input.at[:, lanes], target.at[:, pl.ds(s * 1024, 1024)]))
    for target in (own, other):
        pairs.append((value_tangent, target.at[:, pl.ds(2048, 512)]))
    for k, piece in enumerate((c0, c1, c2, c3)):
        lanes = pl.ds(pl.multiple_of((head ^ k) * 512, 512), 512)
        pairs.append((cotangent.at[:, lanes], piece))
    for copy in copy_all(pairs, semaphores):
        copy.wait()


def square_norm(query_direction, key_tangent, value_tangent, out):
    norm = (
        jnp.sum(jnp.square(query_direction[...].astype(F32)))
        + jnp.sum(jnp.square(key_tangent[...].astype(F32)))
        + jnp.sum(jnp.square(value_tangent[...].astype(F32)))
    )
    out[...] = jnp.full((8, 128), norm, F32)


def absorb(qq, blocks, acc, stats, t, diagonal):
    def two_heads(i, _):
        rows = pl.ds(pl.multiple_of(i * 512, 512), 512)
        both_q = qq[t, rows, :]
        halves = [(block, i) for block in blocks for i in range(2)]
        both_k = jnp.concatenate([block[i, :, 0:256] for block, i in halves], axis=0)
        value = jnp.concatenate([block[i, :, 256:384] for block, i in halves], axis=1)
        value_tan = jnp.concatenate([block[i, :, 384:512] for block, i in halves], axis=1)
        scores = lax.dot_general(
            both_k[:, :128], both_q[:, 128:], ACROSS, preferred_element_type=F32
        )
        tangent = lax.dot_general(both_k, both_q, ACROSS, preferred_element_type=F32)
        if diagonal:
            c = lax.axis_index("c")
            k = lax.broadcasted_iota(jnp.int32, (256, 512), 0)
            r = lax.broadcasted_iota(jnp.int32, (256, 512), 1) % 256
            k = jnp.bitwise_xor(k, c * 128)
            r = jnp.bitwise_xor(r, c * 128)
            scores = jnp.where(k <= r, scores, NEVER)
        top, total, slope = (stats[t, n : n + 1, rows] for n in range(3))
        new_top = jnp.maximum(top, jnp.max(scores, axis=0, keepdims=True))
        decay = jnp.exp2((top - new_top) * SCALE_LOG2)
        weights = jnp.exp2((scores - new_top) * SCALE_LOG2)
        moved = weights * tangent
        stats[t, 0:1, rows] = new_top
        stats[t, 1:2, rows] = total * decay + jnp.sum(weights, axis=0, keepdims=True)
        stats[t, 2:3, rows] = slope * decay + jnp.sum(moved, axis=0, keepdims=True) * SCALE
        weights_b = weights.astype(BF16)
        moved_b = moved.astype(BF16)
        both_v = jnp.concatenate([value, value_tan], axis=0)
        plain = jnp.dot(both_v, weights_b, preferred_element_type=F32)
        turned = jnp.dot(value, moved_b, preferred_element_type=F32)
        acc[t, 0:128, rows] = acc[t, 0:128, rows] * decay + plain[:128]
        acc[t, 128:256, rows] = (
            acc[t, 128:256, rows] * decay + plain[128:] + turned * SCALE
        )
        return 0

    lax.fori_loop(0, 2, two_heads, 0, unroll=2)


def attend_first(q, block, qq, acc, stats, q_held, held, semaphores):
    h, head = lax.axis_index("h"), own_head()
    pairs = [(q, q_held)]
    pairs += [(block.at[pl.ds(2 * f, 2)], held.at[f]) for f in range(2)]
    copies = copy_all(pairs, semaphores)
    acc[...] = jnp.zeros_like(acc)
    line = lax.broadcasted_iota(jnp.int32, (2, 8, 1024), 1)
    stats[...] = jnp.where(line == 0, NEVER, 0.0)
    for copy in copies:
        copy.wait()
    for k in range(4):
        for g in range(4):
            at = g * 256 + (k & 1) * 128
            qq[k >> 1, at : at + 128, :] = q_held[head ^ k, :, g * 256 : (g + 1) * 256]
    absorb(qq, [held.at[0]], acc, stats, 0, True)
    absorb(qq, [held.at[1]], acc, stats, 1, True)

    @pl.when(h == 1)
    def _():
        absorb(qq, [held.at[1]], acc, stats, 0, False)

    @pl.when(h == 0)
    def _():
        absorb(qq, [held.at[0]], acc, stats, 1, False)


def attend(arrivals, qq, acc_in, stats_in, *refs):
    blocks, (acc, stats, held, semaphores) = refs[: len(arrivals)], refs[len(arrivals) :]
    h = lax.axis_index("h")
    z = lax.axis_index("z")
    pairs = []
    for i, ((half, _), block) in enumerate(zip(arrivals, blocks)):
        source = block.at[pl.ds(2 * half, 2)] if block.shape[0] == 4 else block
        pairs.append((source, held.at[i]))
    copies = copy_all(pairs, semaphores)
    acc[...] = acc_in[...]
    stats[...] = stats_in[...]
    earlier = [(z - hops + Z) % Z < z for _, hops in arrivals]
    for copy in copies:
        copy.wait()

    def absorb_when(visible, t, which):
        @pl.when(visible)
        def _():
            absorb(qq, [held.at[i] for i in which], acc, stats, t, False)

    first, second = arrivals[0][0], arrivals[1][0]
    if first == second:
        both = jnp.logical_and(earlier[0], earlier[1])
        absorb_when(both, first, (0, 1))
        absorb_when(jnp.logical_and(earlier[0], jnp.logical_not(both)), first, (0,))
        absorb_when(jnp.logical_and(earlier[1], jnp.logical_not(both)), first, (1,))
        absorb_when((h ^ (1 - first)) == 1, 1 - first, (0, 1))
    else:
        for i, half in enumerate((first, second)):
            absorb_when(earlier[i], half, (i,))
            absorb_when((h ^ (1 - half)) == 1, 1 - half, (i,))


def finish(acc, stats, c0, c1, c2, c3, norm, a0, a1, a2, a3, sums):
    dot = jnp.zeros((128, 128), F32)
    for k, (cot, att) in enumerate(((c0, a0), (c1, a1), (c2, a2), (c3, a3))):
        for g in range(4):
            at = g * 256 + (k & 1) * 128
            rows = slice(at, at + 128)
            total, slope = stats[k >> 1, 1:2, rows], stats[k >> 1, 2:3, rows]
            inverse = 1.0 / total
            output = acc[k >> 1, 0:128, rows] * inverse
            tangent = acc[k >> 1, 128:256, rows] * inverse - slope * inverse * output
            lanes = slice(g * 128, (g + 1) * 128)
            att[:, lanes] = output.T.astype(BF16)
            dot += tangent.T * cot[:, lanes].astype(F32)
    lane = lax.broadcasted_iota(jnp.int32, (8, 128), 1)
    sums[...] = jnp.where(lane == 0, jnp.sum(dot), jnp.where(lane == 1, norm[...], 0.0))


def place(r0, r1, r2, r3, out):
    head = own_head()
    for k, piece in enumerate((r0, r1, r2, r3)):
        lanes = pl.ds(pl.multiple_of((head ^ k) * 512, 512), 512)
        out[:, lanes] = piece[...]


def project(x0, x1, own, other):
    first = lax.axis_index("c") == 0
    tangent = jnp.concatenate([x0[:, 2048:2560], x1[:, 2048:2560]], axis=0)
    for s in range(2):
        for z in range(Z):
            lanes = slice(s * 1024 + z * 128, s * 1024 + (z + 1) * 128)
            rows = jnp.concatenate([x0[:, lanes], x1[:, lanes]], axis=0)
            product = lax.dot_general(
                rows, tangent, (((0,), (0,)), ((), ())), preferred_element_type=F32
            )
            top, bottom = product[:64], product[64:]
            mine = jnp.where(first, top, bottom)
            theirs = jnp.where(first, bottom, top).astype(BF16)
            for y in range(4):
                rows, taken = slice(z * 16, (z + 1) * 16), slice(y * 16, (y + 1) * 16)
                own[s * 4 + y, rows, :] = mine[taken]
                other[s * 4 + y, rows, :] = theirs[taken]


def after(array, *others):
    return lax.optimization_barrier((array,) + others)[0]


def swap(array, k):
    return lax.ppermute(array, ("h", "c"), [(i, i ^ k) for i in range(4)])


def per_device(
    queries, query_direction, keys, key_tangent, values, value_tangent, layer_input, cotangent
):
    queries, query_direction, cotangent = queries[0], query_direction[0], cotangent[0]
    keys, key_tangent, values, value_tangent = keys[0], key_tangent[0], values[0], value_tangent[0]
    layer_input = layer_input[0]

    dma = pltpu.SemaphoreType.DMA
    n_dp = lax.axis_size("y")
    piece = shaped((TOKENS, 512), BF16)
    kv = call(
        pack_keys,
        [piece] * 4,
        [ANY] * 4,
        scratch=[pltpu.VMEM((4, TOKENS, 512), BF16), dma((4,))],
        vmem=LARGE,
    )(keys, key_tangent, values, value_tangent)
    kv1, kv2, kv3 = [swap(kv[k], k) for k in (1, 2, 3)]
    block = jnp.stack([kv[0], kv1, kv2, kv3])

    (q_all,) = call(
        pack_queries,
        [shaped((4, TOKENS, 1024), BF16)],
        [ANY] * 2,
        scratch=[dma((32,))],
        vmem=LARGE,
    )(after(queries, kv[0]), query_direction)
    q_all = lax.all_to_all(after(q_all, block), ("h", "c"), 0, 0, tiled=True)
    x_own, x_other, *cot = call(
        pack_inputs,
        [shaped((TOKENS, 2560), BF16)] * 2 + [shaped((TOKENS, 512), BF16)] * 4,
        [ANY] * 3,
        scratch=[dma((10,))],
        vmem=LARGE,
    )(after(layer_input, block), value_tangent, cotangent)
    (norm,) = call(square_norm, [shaped((8, 128), F32)], [VMEM] * 3)(
        after(query_direction, x_own), key_tangent, value_tangent
    )

    tile_flops = 2 * 6 * 128 * 256 * 1024
    state = [shaped((2, 256, 1024), F32), shaped((2, 8, 1024), F32)]
    up = [(i, (i + 1) % Z) for i in range(Z)]
    down = [(i, (i - 1) % Z) for i in range(Z)]

    def hop(array, route):
        return lax.ppermute(array, "z", route)

    def attend_step(acc, stats, arrivals, blocks):
        return call(
            functools.partial(attend, arrivals),
            state,
            [VMEM] * 3 + [ANY] * len(blocks),
            flops=3 * tile_flops * len(blocks) // 4,
            scratch=[pltpu.VMEM((len(blocks), 2, TOKENS, 512), BF16), dma((len(blocks),))],
            aliases={1: 0, 2: 1},
        )(qq, acc, stats, *blocks)

    def stage(blocks):
        return [hop(blocks[0], up), hop(blocks[1], down)]

    tie = lax.optimization_barrier
    ring1 = stage((block, block))
    *ring1, x_own, x_other, norm = tie((*ring1, x_own, x_other, norm))
    ring2 = stage(ring1)
    qq, acc, stats = call(
        attend_first,
        [shaped((2, 1024, 256), BF16)] + state,
        [ANY] * 2,
        flops=3 * tile_flops,
        scratch=[
            pltpu.VMEM((4, TOKENS, 1024), BF16),
            pltpu.VMEM((2, 2, TOKENS, 512), BF16),
            dma((3,)),
        ],
    )(q_all, block)
    x_other = swap(after(x_other, q_all), 2)
    acc, stats = attend_step(acc, stats, ((0, 1), (0, -1)), ring1)
    *ring2, acc, stats, x_other = tie((*ring2, acc, stats, x_other))

    ring3 = stage(ring2)
    own, other = call(
        project,
        [shaped((Z, 128, 512), F32), shaped((Z, 128, 512), BF16)],
        [VMEM] * 2,
        flops=2 * 256 * 2048 * 512,
    )(x_own, x_other)
    acc, other = tie((acc, other))
    theirs = swap(other, 1)
    cot = [cot[0]] + [swap(after(cot[k], x_other), k) for k in (1, 2, 3)]
    acc, stats = attend_step(acc, stats, ((1, 1), (1, -1)), ring1)
    pair = (own + theirs.astype(F32)).astype(BF16)
    acc, pair = tie((acc, pair))
    parts = lax.all_to_all(pair, ("s", "y"), 0, 0, tiled=True)
    acc, stats = attend_step(acc, stats, ((0, 2), (0, -2)), ring2)
    ring3, acc, stats, cot = tie((ring3, acc, stats, cot))

    ring4 = hop(ring3[0], up)
    acc, stats = attend_step(acc, stats, ((1, 2), (1, -2)), ring2)
    acc, stats = attend_step(acc, stats, ((0, 3), (0, -3)), ring3)
    ring4, acc, stats = tie((ring4, acc, stats))

    acc, stats = attend_step(acc, stats, ((1, 3), (1, -3)), ring3)
    acc, stats = attend_step(acc, stats, ((0, 4), (1, 4)), (ring4, ring4))
    acc = after(acc, parts)

    *att, sums = call(
        finish, [shaped((TOKENS, 512), BF16)] * 4 + [shaped((8, 128), F32)], [VMEM] * 7
    )(acc, stats, *cot, norm)
    sums = sums[:1] + swap(sums[:1], 1)
    att = [att[0]] + [swap(after(att[k], sums), k) for k in (1, 2, 3)]
    (attended,) = call(place, [shaped((TOKENS, 2048), BF16)], [VMEM] * 4)(*att)

    every = lax.all_to_all(
        jnp.broadcast_to(sums, (32 * n_dp, 128)), ("s", "h", "z", "y"), 0, 0, tiled=True
    )
    every = after(every, attended).reshape(2, 2 * Z, n_dp, 128).sum(axis=1)
    derivative, tangent_norm = every[..., 0], every[..., 1]
    block_count = SEQUENCE_LENGTH * (QUERY_HEADS + 2 * KEY_VALUE_HEADS) * HEAD_SIZE
    factor = derivative / (
        (tangent_norm / block_count + 1e-06)
        * SEQUENCE_LENGTH
        * math.sqrt(QUERY_HEADS * HEAD_SIZE)
    )
    shares = jnp.sum(factor.reshape(8, 1, 1) * parts.astype(F32), axis=0)
    shares = lax.all_to_all(shares.astype(BF16), "z", 0, 0, tiled=True)
    value_update = jnp.sum(shares.reshape(Z, 16, 512).astype(F32), axis=0)
    return attended[None], value_update


def solution(mesh):
    n_dp = mesh.shape["dp"]
    fine = Mesh(mesh.devices.reshape(2, 2, Z, 2, n_dp), ("s", "h", "z", "c", "y"))
    along = ("s", "h", "z", "c")
    placed = P("y", along, None)
    return jax.shard_map(
        per_device,
        mesh=fine,
        in_specs=(placed,) * 8,
        out_specs=(placed, P(along + ("y",), None)),
        check_vma=False,
    )
```

```python
import functools
import math

import jax
import jax.numpy as jnp
from jax import lax
from jax.experimental import pallas as pl
from jax.experimental.pallas import tpu as pltpu
from jax.sharding import Mesh, PartitionSpec as P

QUERY_HEADS = 16
KEY_VALUE_HEADS = 4
HEAD_SIZE = 128
GROUP_HEADS = 4
SEQUENCE_LENGTH = 4096
Z = 8
TOKENS = 128
SCALE = 1.0 / math.sqrt(HEAD_SIZE)
SCALE_LOG2 = SCALE * math.log2(math.e)
F32 = jnp.float32
BF16 = jnp.bfloat16
VMEM = pl.BlockSpec(memory_space=pltpu.VMEM)
ANY = pl.BlockSpec(memory_space=pltpu.HBM)
NEVER = -1e30
LARGE = 60 << 20
ACROSS = (((1,), (1,)), ((), ()))


def shaped(shape, dtype):
    return jax.ShapeDtypeStruct(shape, dtype)


def call(kernel, outs, ins, flops=0, scratch=(), out_specs=None, aliases=None, vmem=24 << 20):
    return pl.pallas_call(
        kernel,
        out_shape=outs,
        in_specs=ins,
        out_specs=out_specs or [VMEM] * len(outs),
        scratch_shapes=list(scratch),
        input_output_aliases=aliases or {},
        compiler_params=pltpu.CompilerParams(vmem_limit_bytes=vmem),
        cost_estimate=pl.CostEstimate(flops=flops, bytes_accessed=0, transcendentals=0),
    )


def copy_all(pairs, semaphores):
    copies = [
        pltpu.make_async_copy(source, target, semaphores.at[i])
        for i, (source, target) in enumerate(pairs)
    ]
    for copy in copies:
        copy.start()
    return copies


def own_head():
    return 2 * lax.axis_index("h") + lax.axis_index("c")


def pack_keys(keys, key_tangent, values, value_tangent, *refs):
    pieces, (held, semaphores) = refs[:4], refs[4:]
    head = own_head()
    sources = (keys, key_tangent, values, value_tangent)
    for copy in copy_all([(source, held.at[i]) for i, source in enumerate(sources)], semaphores):
        copy.wait()
    for k in range(4):
        lanes = pl.ds(pl.multiple_of((head ^ k) * HEAD_SIZE, HEAD_SIZE), HEAD_SIZE)
        pieces[k][:, 0:128] = held[0, :, lanes]
        pieces[k][:, 128:256] = held[1, :, lanes]
        pieces[k][:, 256:384] = held[2, :, lanes].T
        pieces[k][:, 384:512] = held[3, :, lanes].T


def pack_queries(queries, query_direction, q, semaphores):
    pairs = []
    for j in range(4):
        for g in range(4):
            lanes = pl.ds(j * 512 + g * 128, 128)
            pairs.append((query_direction.at[:, lanes], q.at[j, :, pl.ds(g * 256, 128)]))
            pairs.append((queries.at[:, lanes], q.at[j, :, pl.ds(g * 256 + 128, 128)]))
    for copy in copy_all(pairs, semaphores):
        copy.wait()


def pack_inputs(layer_input, value_tangent, cotangent, own, other, c0, c1, c2, c3, semaphores):
    h, head = lax.axis_index("h"), own_head()
    pairs = []
    for s in range(2):
        for target, half in ((own, h), (other, 1 - h)):
            lanes = pl.ds(pl.multiple_of(s * 2048 + half * 1024, 1024), 1024)
            pairs.append((layer_input.at[:, lanes], target.at[:, pl.ds(s * 1024, 1024)]))
    for target in (own, other):
        pairs.append((value_tangent, target.at[:, pl.ds(2048, 512)]))
    for k, piece in enumerate((c0, c1, c2, c3)):
        lanes = pl.ds(pl.multiple_of((head ^ k) * 512, 512), 512)
        pairs.append((cotangent.at[:, lanes], piece))
    for copy in copy_all(pairs, semaphores):
        copy.wait()


def square_norm(query_direction, key_tangent, value_tangent, out):
    norm = (
        jnp.sum(jnp.square(query_direction[...].astype(F32)))
        + jnp.sum(jnp.square(key_tangent[...].astype(F32)))
        + jnp.sum(jnp.square(value_tangent[...].astype(F32)))
    )
    out[...] = jnp.full((8, 128), norm, F32)


def absorb(qq, blocks, acc, stats, t, diagonal):
    def two_heads(i, _):
        rows = pl.ds(pl.multiple_of(i * 512, 512), 512)
        both_q = qq[t, rows, :]
        halves = [(block, i) for block in blocks for i in range(2)]
        both_k = jnp.concatenate([block[i, :, 0:256] for block, i in halves], axis=0)
        value = jnp.concatenate([block[i, :, 256:384] for block, i in halves], axis=1)
        value_tan = jnp.concatenate([block[i, :, 384:512] for block, i in halves], axis=1)
        scores = lax.dot_general(
            both_k[:, :128], both_q[:, 128:], ACROSS, preferred_element_type=F32
        )
        tangent = lax.dot_general(both_k, both_q, ACROSS, preferred_element_type=F32)
        if diagonal:
            c = lax.axis_index("c")
            k = lax.broadcasted_iota(jnp.int32, (256, 512), 0)
            r = lax.broadcasted_iota(jnp.int32, (256, 512), 1) % 256
            k = jnp.bitwise_xor(k, c * 128)
            r = jnp.bitwise_xor(r, c * 128)
            scores = jnp.where(k <= r, scores, NEVER)
        top, total, slope = (stats[t, n : n + 1, rows] for n in range(3))
        new_top = jnp.maximum(top, jnp.max(scores, axis=0, keepdims=True))
        decay = jnp.exp2((top - new_top) * SCALE_LOG2)
        weights = jnp.exp2((scores - new_top) * SCALE_LOG2)
        moved = weights * tangent
        stats[t, 0:1, rows] = new_top
        stats[t, 1:2, rows] = total * decay + jnp.sum(weights, axis=0, keepdims=True)
        stats[t, 2:3, rows] = slope * decay + jnp.sum(moved, axis=0, keepdims=True) * SCALE
        weights_b = weights.astype(BF16)
        moved_b = moved.astype(BF16)
        both_v = jnp.concatenate([value, value_tan], axis=0)
        plain = jnp.dot(both_v, weights_b, preferred_element_type=F32)
        turned = jnp.dot(value, moved_b, preferred_element_type=F32)
        acc[t, 0:128, rows] = acc[t, 0:128, rows] * decay + plain[:128]
        acc[t, 128:256, rows] = (
            acc[t, 128:256, rows] * decay + plain[128:] + turned * SCALE
        )
        return 0

    lax.fori_loop(0, 2, two_heads, 0, unroll=2)


def attend_first(q, block, qq, acc, stats, q_held, held, semaphores):
    h, head = lax.axis_index("h"), own_head()
    pairs = [(q, q_held)]
    pairs += [(block.at[pl.ds(2 * f, 2)], held.at[f]) for f in range(2)]
    copies = copy_all(pairs, semaphores)
    acc[...] = jnp.zeros_like(acc)
    line = lax.broadcasted_iota(jnp.int32, (2, 8, 1024), 1)
    stats[...] = jnp.where(line == 0, NEVER, 0.0)
    for copy in copies:
        copy.wait()
    for k in range(4):
        for g in range(4):
            at = g * 256 + (k & 1) * 128
            qq[k >> 1, at : at + 128, :] = q_held[head ^ k, :, g * 256 : (g + 1) * 256]
    absorb(qq, [held.at[0]], acc, stats, 0, True)
    absorb(qq, [held.at[1]], acc, stats, 1, True)

    @pl.when(h == 1)
    def _():
        absorb(qq, [held.at[1]], acc, stats, 0, False)

    @pl.when(h == 0)
    def _():
        absorb(qq, [held.at[0]], acc, stats, 1, False)


def attend(arrivals, qq, acc_in, stats_in, *refs):
    blocks, (acc, stats, held, semaphores) = refs[: len(arrivals)], refs[len(arrivals) :]
    h = lax.axis_index("h")
    z = lax.axis_index("z")
    pairs = []
    for i, ((half, _), block) in enumerate(zip(arrivals, blocks)):
        source = block.at[pl.ds(2 * half, 2)] if block.shape[0] == 4 else block
        pairs.append((source, held.at[i]))
    copies = copy_all(pairs, semaphores)
    acc[...] = acc_in[...]
    stats[...] = stats_in[...]
    earlier = [(z - hops + Z) % Z < z for _, hops in arrivals]
    for copy in copies:
        copy.wait()

    def absorb_when(visible, t, which):
        @pl.when(visible)
        def _():
            absorb(qq, [held.at[i] for i in which], acc, stats, t, False)

    first, second = arrivals[0][0], arrivals[1][0]
    if first == second:
        both = jnp.logical_and(earlier[0], earlier[1])
        absorb_when(both, first, (0, 1))
        absorb_when(jnp.logical_and(earlier[0], jnp.logical_not(both)), first, (0,))
        absorb_when(jnp.logical_and(earlier[1], jnp.logical_not(both)), first, (1,))
        absorb_when((h ^ (1 - first)) == 1, 1 - first, (0, 1))
    else:
        for i, half in enumerate((first, second)):
            absorb_when(earlier[i], half, (i,))
            absorb_when((h ^ (1 - half)) == 1, 1 - half, (i,))


def finish(acc, stats, c0, c1, c2, c3, norm, a0, a1, a2, a3, sums):
    dot = jnp.zeros((128, 128), F32)
    for k, (cot, att) in enumerate(((c0, a0), (c1, a1), (c2, a2), (c3, a3))):
        for g in range(4):
            at = g * 256 + (k & 1) * 128
            rows = slice(at, at + 128)
            total, slope = stats[k >> 1, 1:2, rows], stats[k >> 1, 2:3, rows]
            inverse = 1.0 / total
            output = acc[k >> 1, 0:128, rows] * inverse
            tangent = acc[k >> 1, 128:256, rows] * inverse - slope * inverse * output
            lanes = slice(g * 128, (g + 1) * 128)
            att[:, lanes] = output.T.astype(BF16)
            dot += tangent.T * cot[:, lanes].astype(F32)
    lane = lax.broadcasted_iota(jnp.int32, (8, 128), 1)
    sums[...] = jnp.where(lane == 0, jnp.sum(dot), jnp.where(lane == 1, norm[...], 0.0))


def place(r0, r1, r2, r3, out):
    head = own_head()
    for k, piece in enumerate((r0, r1, r2, r3)):
        lanes = pl.ds(pl.multiple_of((head ^ k) * 512, 512), 512)
        out[:, lanes] = piece[...]


def project(x0, x1, own, other):
    first = lax.axis_index("c") == 0
    tangent = jnp.concatenate([x0[:, 2048:2560], x1[:, 2048:2560]], axis=0)
    for s in range(2):
        for z in range(Z):
            lanes = slice(s * 1024 + z * 128, s * 1024 + (z + 1) * 128)
            rows = jnp.concatenate([x0[:, lanes], x1[:, lanes]], axis=0)
            product = lax.dot_general(
                rows, tangent, (((0,), (0,)), ((), ())), preferred_element_type=F32
            )
            top, bottom = product[:64], product[64:]
            mine = jnp.where(first, top, bottom)
            theirs = jnp.where(first, bottom, top).astype(BF16)
            for y in range(4):
                rows, taken = slice(z * 16, (z + 1) * 16), slice(y * 16, (y + 1) * 16)
                own[s * 4 + y, rows, :] = mine[taken]
                other[s * 4 + y, rows, :] = theirs[taken]


def after(array, *others):
    return lax.optimization_barrier((array,) + others)[0]


def swap(array, k):
    return lax.ppermute(array, ("h", "c"), [(i, i ^ k) for i in range(4)])


def per_device(
    queries, query_direction, keys, key_tangent, values, value_tangent, layer_input, cotangent
):
    queries, query_direction, cotangent = queries[0], query_direction[0], cotangent[0]
    keys, key_tangent, values, value_tangent = keys[0], key_tangent[0], values[0], value_tangent[0]
    layer_input = layer_input[0]

    dma = pltpu.SemaphoreType.DMA
    n_dp = lax.axis_size("y")
    piece = shaped((TOKENS, 512), BF16)
    kv = call(
        pack_keys,
        [piece] * 4,
        [ANY] * 4,
        scratch=[pltpu.VMEM((4, TOKENS, 512), BF16), dma((4,))],
        vmem=LARGE,
    )(keys, key_tangent, values, value_tangent)
    kv1, kv2, kv3 = [swap(kv[k], k) for k in (1, 2, 3)]
    block = jnp.stack([kv[0], kv1, kv2, kv3])

    (q_all,) = call(
        pack_queries,
        [shaped((4, TOKENS, 1024), BF16)],
        [ANY] * 2,
        scratch=[dma((32,))],
        vmem=LARGE,
    )(after(queries, kv[0]), query_direction)
    q_all = lax.all_to_all(after(q_all, block), ("h", "c"), 0, 0, tiled=True)
    x_own, x_other, *cot = call(
        pack_inputs,
        [shaped((TOKENS, 2560), BF16)] * 2 + [shaped((TOKENS, 512), BF16)] * 4,
        [ANY] * 3,
        scratch=[dma((10,))],
        vmem=LARGE,
    )(after(layer_input, block), value_tangent, cotangent)
    (norm,) = call(square_norm, [shaped((8, 128), F32)], [VMEM] * 3)(
        after(query_direction, x_own), key_tangent, value_tangent
    )

    tile_flops = 2 * 6 * 128 * 256 * 1024
    state = [shaped((2, 256, 1024), F32), shaped((2, 8, 1024), F32)]
    up = [(i, (i + 1) % Z) for i in range(Z)]
    down = [(i, (i - 1) % Z) for i in range(Z)]

    def hop(array, route):
        return lax.ppermute(array, "z", route)

    def attend_step(acc, stats, arrivals, blocks):
        return call(
            functools.partial(attend, arrivals),
            state,
            [VMEM] * 3 + [ANY] * len(blocks),
            flops=3 * tile_flops * len(blocks) // 4,
            scratch=[pltpu.VMEM((len(blocks), 2, TOKENS, 512), BF16), dma((len(blocks),))],
            aliases={1: 0, 2: 1},
        )(qq, acc, stats, *blocks)

    def stage(blocks):
        return [hop(blocks[0], up), hop(blocks[1], down)]

    tie = lax.optimization_barrier
    ring1 = stage((block, block))
    *ring1, x_own, x_other, norm = tie((*ring1, x_own, x_other, norm))
    ring2 = stage(ring1)
    qq, acc, stats = call(
        attend_first,
        [shaped((2, 1024, 256), BF16)] + state,
        [ANY] * 2,
        flops=3 * tile_flops,
        scratch=[
            pltpu.VMEM((4, TOKENS, 1024), BF16),
            pltpu.VMEM((2, 2, TOKENS, 512), BF16),
            dma((3,)),
        ],
    )(q_all, block)
    x_other = swap(after(x_other, q_all), 2)
    acc, stats = attend_step(acc, stats, ((0, 1), (0, -1)), ring1)
    *ring2, acc, stats, x_other = tie((*ring2, acc, stats, x_other))

    ring3 = stage(ring2)
    own, other = call(
        project,
        [shaped((Z, 128, 512), F32), shaped((Z, 128, 512), BF16)],
        [VMEM] * 2,
        flops=2 * 256 * 2048 * 512,
    )(x_own, x_other)
    acc, other = tie((acc, other))
    theirs = swap(other, 1)
    cot = [cot[0]] + [swap(after(cot[k], x_other), k) for k in (1, 2, 3)]
    acc, stats = attend_step(acc, stats, ((1, 1), (1, -1)), ring1)
    pair = (own + theirs.astype(F32)).astype(BF16)
    acc, pair, cot = tie((acc, pair, cot))
    parts = lax.all_to_all(pair, ("s", "y"), 0, 0, tiled=True)
    acc, stats = attend_step(acc, stats, ((0, 2), (0, -2)), ring2)
    ring3, acc, stats = tie((ring3, acc, stats))

    ring4 = hop(ring3[0], up)
    acc, stats = attend_step(acc, stats, ((1, 2), (1, -2)), ring2)
    acc, stats = attend_step(acc, stats, ((0, 3), (0, -3)), ring3)
    ring4, acc, stats = tie((ring4, acc, stats))

    acc, stats = attend_step(acc, stats, ((1, 3), (1, -3)), ring3)
    acc, stats = attend_step(acc, stats, ((0, 4), (1, 4)), (ring4, ring4))
    acc = after(acc, parts)

    *att, sums = call(
        finish, [shaped((TOKENS, 512), BF16)] * 4 + [shaped((8, 128), F32)], [VMEM] * 7
    )(acc, stats, *cot, norm)
    sums = sums[:1] + swap(sums[:1], 1)
    att = [att[0]] + [swap(after(att[k], sums), k) for k in (1, 2, 3)]
    (attended,) = call(place, [shaped((TOKENS, 2048), BF16)], [VMEM] * 4)(*att)

    every = lax.all_to_all(
        jnp.broadcast_to(sums, (32 * n_dp, 128)), ("s", "h", "z", "y"), 0, 0, tiled=True
    )
    every = after(every, attended).reshape(2, 2 * Z, n_dp, 128).sum(axis=1)
    derivative, tangent_norm = every[..., 0], every[..., 1]
    block_count = SEQUENCE_LENGTH * (QUERY_HEADS + 2 * KEY_VALUE_HEADS) * HEAD_SIZE
    factor = derivative / (
        (tangent_norm / block_count + 1e-06)
        * SEQUENCE_LENGTH
        * math.sqrt(QUERY_HEADS * HEAD_SIZE)
    )
    shares = jnp.sum(factor.reshape(8, 1, 1) * parts.astype(F32), axis=0)
    shares = lax.all_to_all(shares.astype(BF16), "z", 0, 0, tiled=True)
    value_update = jnp.sum(shares.reshape(Z, 16, 512).astype(F32), axis=0)
    return attended[None], value_update


def solution(mesh):
    n_dp = mesh.shape["dp"]
    fine = Mesh(mesh.devices.reshape(2, 2, Z, 2, n_dp), ("s", "h", "z", "c", "y"))
    along = ("s", "h", "z", "c")
    placed = P("y", along, None)
    return jax.shard_map(
        per_device,
        mesh=fine,
        in_specs=(placed,) * 8,
        out_specs=(placed, P(along + ("y",), None)),
        check_vma=False,
    )
```
